32 devices in a mesh: fine: 4 (over z), coarse: 2 (over y), comp: 4 (over x, core).
Axes of the slice: x: 2, y: 2, z: 4, core: 2. Of those that a mesh axis runs over, the one named last changes fastest.
Arguments:
- a_vals: bfloat16 [384, 64, 448], P(('fine', 'coarse', 'comp')), may hold values from -0.25 to 0.25
- a_cols: int32 [384, 7], P(('fine', 'coarse', 'comp')), may hold values from 0 to 27, as said below
- p_vals: bfloat16 [384, 64, 256], P(('fine', 'coarse', 'comp')), may hold values from -1 to 1
- p_cols: int32 [384, 4], P(('fine', 'coarse', 'comp')), may hold values from 0 to 7, as said below
- gp_cols: int32 [512, 4], P(('fine', 'coarse', 'comp')), may hold values from 0 to 15, as said below
- send_list: int32 [512], P(('fine', 'coarse', 'comp')), may hold values from 0 to 11
Outputs:
- coarse_op: float32 [4, 512, 4, 1024], P('fine', 'coarse', 'comp')
The draws below stay inside these ranges and needn't reach their ends.
Inputs may be any that keep to these rules, and one draw needn't show every extreme that they name: `a_cols`: A value e below 12 names local row e of the same device, a value 12 + s names ghost slot s; the first entry of each row is the row itself, and every ghost slot of a device is named by at least one entry of its rows. `p_cols`: the 4 entries of a row are distinct. `gp_cols`: the 4 entries of a row are distinct.
All inputs are finite; a program needn't handle non-finite values.
Results may differ from the reference program's by a relative error of at most 0.0029.
Values may be sent and summed in bfloat16 or wider, within the bound.
A program may use at most 64 MiB of HBM per device.

```python
import jax
import jax.numpy as jnp
from jax import lax

B = 64
KA = 7
KP = 4
NC = 8
EXT = 8
G = 1
NBD = 12
NCW = 16
GDEV = 16
NB = 384
NGHOST = 512
N_FINE = 4
N_COARSE = 2
N_COMP = 4
DEVICES = 32


def draw_a_cols(key, part):
    head_key, tail_key = jax.random.split(key)
    entry_count = NBD * (KA - 1)
    device_keys = jax.random.split(head_key, DEVICES)
    orders = jax.vmap(lambda single_key: jax.random.permutation(single_key, entry_count))(device_keys)
    nearby = jax.random.randint(tail_key, (DEVICES, entry_count), 0, NBD)
    others = jnp.where(orders < GDEV, NBD + orders, nearby).astype(jnp.int32).reshape(DEVICES, NBD, KA - 1)
    itself = jnp.broadcast_to(jnp.arange(NBD, dtype=jnp.int32)[None, :, None], (DEVICES, NBD, 1))
    return jnp.concatenate([itself, others], axis=2).reshape(NB, KA)


def distinct_columns(key, row_count, pick_count, span_width):
    row_keys = jax.random.split(key, row_count)
    picked = jax.vmap(lambda single_key: jax.random.permutation(single_key, span_width)[:pick_count])(row_keys)
    return picked.astype(jnp.int32)


def draw_p_cols(key, part):
    return distinct_columns(jax.random.fold_in(key, 11), NB, KP, NC)


def draw_gp_cols(key, part):
    return distinct_columns(jax.random.fold_in(key, 23), NGHOST, KP, NCW)


def place_ends(values, key, smallest, largest):
    shape = values.shape
    place = [jax.random.randint(jax.random.fold_in(key, axis), (), 0, shape[axis]) for axis in range(len(shape))]
    values = values.at[tuple(place)].set(smallest)
    longest = shape.index(max(shape))
    place[longest] = (place[longest] + 1) % shape[longest]
    return values.at[tuple(place)].set(largest)


def block_levels(key, dims, cuts, least, top_value):
    level, own = 1.0, jax.random.fold_in(key, 6)
    for dim, blocks in cuts:
        draws = jnp.exp(jax.random.uniform(jax.random.fold_in(own, dim), (blocks,), jnp.float32, least / len(cuts), top_value / len(cuts)))
        level = level * jnp.repeat(draws, dims[dim] // blocks).reshape([-1 if axis == dim else 1 for axis in range(len(dims))])
    return level


def noise(stream_key, shape, scale, reach, pieces=(), held_as=jnp.bfloat16):
    drawn = scale * jax.random.normal(stream_key, shape, jnp.float32)
    if pieces:
        drawn = drawn * block_levels(stream_key, shape, pieces, -0.22, 0.18)
    return jnp.clip(drawn, -reach, reach).astype(held_as)


def setup_inputs(seed: int = 0) -> dict:
    arg_keys = jax.random.split(jax.random.key(seed), 7)
    return {
        "a_vals": noise(arg_keys[0], (NB, B, KA * B), (B * KA) ** -0.5, 0.25, ((0, 32),)),
        "a_cols": draw_a_cols(jax.random.fold_in(arg_keys[6], 71), 0),
        "p_vals": noise(arg_keys[2], (NB, B, KP * B), 0.17, 1.0, ((0, 32),)),
        "p_cols": draw_p_cols(jax.random.fold_in(arg_keys[6], 71), 0),
        "gp_cols": draw_gp_cols(jax.random.fold_in(arg_keys[6], 71), 0),
        "send_list": place_ends(jax.random.randint(arg_keys[5], (NGHOST,), 0, NBD), jax.random.fold_in(arg_keys[5], 1), 0, NBD - 1).astype(jnp.int32),
    }


def local_terms(a_rows, a_index, p_rows, p_index, ghosts, g_index):
    block_rows = a_rows.shape[0]
    block_size = a_rows.shape[1]
    pick_count = p_index.shape[1]
    link_count = a_index.shape[1]
    columns_all = NC + EXT
    sources = jnp.concatenate([p_rows, ghosts], axis=0)
    source_cols = jnp.concatenate([p_index, g_index], axis=0).astype(jnp.int32)
    fetched = jnp.take(sources, a_index, axis=0)
    fetched_cols = jnp.take(source_cols, a_index, axis=0)
    column_ids = jnp.arange(columns_all, dtype=jnp.int32)
    placing = (fetched_cols[:, :, :, None] == column_ids[None, None, None, :]).astype(jnp.float32)
    a_split = a_rows.reshape(block_rows, block_size, link_count, block_size)
    terms = jnp.einsum("riam,ramn->rain", a_split.astype(jnp.float32), fetched.astype(jnp.float32))
    terms = terms.reshape(block_rows, block_size, link_count, pick_count, block_size)
    applied = jnp.einsum("rakc,riakj->ricj", placing, terms, precision=lax.Precision.HIGHEST)
    prod_rows = applied.astype(jnp.bfloat16).reshape(block_rows * block_size, columns_all * block_size)
    own_rows = p_rows.reshape(block_rows, block_size, pick_count, block_size)
    owned_ids = jnp.arange(NC, dtype=jnp.int32)
    spread = jnp.zeros((block_rows, block_size, NC, block_size), jnp.bfloat16)
    for pick in range(pick_count):
        hits = p_index[:, pick, None] == owned_ids[None, :]
        spread = jnp.where(hits[:, None, :, None], own_rows[:, :, pick, None, :], spread)
    spread = spread.reshape(block_rows * block_size, NC * block_size)
    return spread, prod_rows


def contract(spread, prod_rows):
    return lax.dot_general(spread, prod_rows, (((0,), (0,)), ((), ())), preferred_element_type=jnp.float32)


def reference(a_vals, a_cols, p_vals, p_cols, gp_cols, send_list):
    fine_n, coarse_n, comp_n = N_FINE, N_COARSE, N_COMP
    a_all = a_vals.reshape(fine_n, coarse_n, comp_n, NBD, B, KA * B)
    p_all = p_vals.reshape(fine_n, coarse_n, comp_n, NBD, B, KP * B)
    ac_all = a_cols.reshape(fine_n, coarse_n, comp_n, NBD, KA)
    pc_all = p_cols.reshape(fine_n, coarse_n, comp_n, NBD, KP)
    gc_all = gp_cols.reshape(fine_n, coarse_n, comp_n, GDEV, KP)
    wanted = jnp.transpose(send_list.reshape(fine_n, coarse_n, comp_n, fine_n, comp_n, G), (3, 1, 4, 0, 2, 5))
    fine_src = jnp.arange(fine_n, dtype=jnp.int32)[:, None, None]
    comp_src = jnp.arange(comp_n, dtype=jnp.int32)[None, :, None]

    def device_term(fine_idx, coarse_idx, comp_idx):
        ghosts = p_all[fine_src, coarse_idx, comp_src, wanted[fine_idx, coarse_idx, comp_idx]].reshape(GDEV, B, KP * B)
        spread, prod_rows = local_terms(a_all[fine_idx, coarse_idx, comp_idx], ac_all[fine_idx, coarse_idx, comp_idx], p_all[fine_idx, coarse_idx, comp_idx], pc_all[fine_idx, coarse_idx, comp_idx], ghosts, gc_all[fine_idx, coarse_idx, comp_idx])
        return contract(spread, prod_rows)

    def subdomain(index):
        fine_idx = index // comp_n
        comp_idx = index % comp_n

        def add_term(total, coarse_idx):
            return total + device_term(fine_idx, coarse_idx, comp_idx), None

        total, _ = lax.scan(add_term, jnp.zeros((NC * B, NCW * B), jnp.float32), jnp.arange(coarse_n, dtype=jnp.int32))
        return total

    blocks = lax.map(subdomain, jnp.arange(fine_n * comp_n, dtype=jnp.int32))
    return jnp.transpose(blocks.reshape(fine_n, comp_n, NC * B, NCW * B), (0, 2, 1, 3))
```

```python
import functools

import jax
import jax.numpy as jnp
from jax import lax
from jax.experimental import pallas as pl
from jax.experimental.pallas import tpu as pltpu
from jax.sharding import PartitionSpec as P

NC = 8
EXT = 8
MESH = pl.DeviceIdType.MESH


def doubled(pair, low):
    turned = pltpu.roll(pair, 64, 1)
    return jnp.where(low, pair, turned), jnp.where(low, turned, pair)


def placed(tiles, ids, columns):
    out = jnp.zeros(tiles[0].shape, jnp.float32)
    for tile, column in zip(tiles, columns):
        out = jnp.where(ids == column, tile, out)
    return out


def kernel(
    shape, a_ref, p_ref, a_cols, p_cols, gp_cols, send_list, out_ref,
    staging, sources, terms, spread, total, prod, outgoing, incoming,
    send_sem, recv_sem, part_send, part_recv,
):
    n_fine, n_coarse, n_comp, per_peer = shape
    block_rows, block, _ = a_ref.shape
    links = a_cols.shape[1]
    picks = p_cols.shape[1]
    group = n_comp * per_peer
    rows = NC * block // n_coarse
    columns = (NC + EXT) * block
    strips = columns // 256
    f, c, m = lax.axis_index("fine"), lax.axis_index("coarse"), lax.axis_index("comp")
    me = f * n_comp + m

    barrier = pltpu.get_barrier_semaphore()
    far = [(df, dm) for t in range(n_fine) for df in [(n_fine // 2 + t) % n_fine]
           for dm in range(n_comp) if df or dm]
    for df, dm in far:
        pl.semaphore_signal(
            barrier, inc=1, device_id_type=MESH,
            device_id=(lax.rem(f + df, n_fine), c, lax.rem(m + dm, n_comp)),
        )
    for dc in range(1, n_coarse):
        pl.semaphore_signal(
            barrier, inc=1, device_id_type=MESH, device_id=(f, lax.rem(c + dc, n_coarse), m)
        )

    def stage(slot, carry):
        staging[slot] = p_ref[send_list[slot]]
        return carry

    lax.fori_loop(0, n_fine * group, stage, 0)
    pl.semaphore_wait(barrier, len(far) + n_coarse - 1)

    def ghost_copy(peer_f, peer_m, to_slot):
        peer = peer_f * n_comp + peer_m
        return pltpu.make_async_remote_copy(
            src_ref=staging.at[pl.ds(peer * per_peer, per_peer)],
            dst_ref=sources.at[pl.ds(block_rows + to_slot * per_peer, per_peer)],
            send_sem=send_sem.at[peer],
            recv_sem=recv_sem.at[to_slot],
            device_id=(peer_f, c, peer_m),
            device_id_type=MESH,
        )

    for df, dm in far:
        ghost_copy(lax.rem(f + df, n_fine), lax.rem(m + dm, n_comp), me).start()
    for g in range(per_peer):
        sources[block_rows + me * per_peer + g] = staging[me * per_peer + g]

    lane = lax.broadcasted_iota(jnp.int32, (block, 128), 1)
    low = lane < block
    upper = jnp.where(low, 0, 1)

    def split_tiles(value, low):
        tiles = []
        for k in range(picks // 2):
            tiles.extend(doubled(value[:, k * 128:(k + 1) * 128].astype(jnp.float32), low))
        return tiles

    def local_pair(pair, carry):
        halves = []
        for side in range(2):
            row = pair * 2 + side
            value = p_ref[row]
            sources[row] = value
            tiles = split_tiles(value, low)
            ids = [p_cols[row, k] for k in range(picks)]
            halves.append([placed(tiles, upper + 2 * i, ids) for i in range(NC // 2)])
        where = pl.ds(pl.multiple_of(pair * 128, 128), 128)
        for i in range(NC // 2):
            both = jnp.concatenate([halves[0][i], halves[1][i]], axis=0)
            spread[i * 128:(i + 1) * 128, where] = both.T.astype(jnp.bfloat16)
        return carry

    lax.fori_loop(0, block_rows // 2, local_pair, 0)

    for df, dm in reversed(far):
        peer_f, peer_m = lax.rem(f + df, n_fine), lax.rem(m + dm, n_comp)
        ghost_copy(peer_f, peer_m, peer_f * n_comp + peer_m).wait_recv()

    half = block // 2
    low_half = lax.broadcasted_iota(jnp.int32, (half, 128), 1) < block
    upper_half = jnp.where(low_half, 0, 1)

    def fine_row(row, side):
        entries = [a_cols[row, a] for a in range(links)]
        for a in range(links):
            term = jnp.dot(
                a_ref[row, :, a * block:(a + 1) * block], sources[entries[a]],
                preferred_element_type=jnp.float32,
            )
            for h in range(picks // 2):
                terms[side, h, pl.ds(a * block, block), :] = term[:, h * 128:(h + 1) * 128]
        ids = [
            [
                jnp.where(
                    e < block_rows,
                    p_cols[jnp.minimum(e, block_rows - 1), k],
                    gp_cols[jnp.maximum(e - block_rows, 0), k],
                )
                for k in range(picks)
            ]
            for e in entries
        ]
        for part in range(2):
            sums = [None] * (columns // 128)
            for a in range(links):
                tiles = []
                for h in range(picks // 2):
                    tiles.extend(doubled(
                        terms[side, h, pl.ds(part * half * links + a, half, stride=links), :], low_half
                    ))
                for j in range(columns // 128):
                    here = placed(tiles, upper_half + 2 * j, ids[a])
                    sums[j] = here if sums[j] is None else sums[j] + here
            for j in range(columns // 128):
                prod[pl.ds(row * block + part * half, half), j * 128:(j + 1) * 128] = sums[j].astype(jnp.bfloat16)

    def fine_pair(pair, carry):
        for side in range(2):
            fine_row(pair * 2 + side, side)
        return carry

    lax.fori_loop(0, block_rows // 2, fine_pair, 0)

    def part_copy(dc, strip):
        return pltpu.make_async_remote_copy(
            src_ref=outgoing.at[dc - 1, strip],
            dst_ref=incoming.at[dc - 1, strip],
            send_sem=part_send.at[dc - 1, strip],
            recv_sem=part_recv.at[dc - 1, strip],
            device_id=(f, lax.rem(c + dc, n_coarse), m),
            device_id_type=MESH,
        )

    def contract(owner, at):
        mine = pl.ds(pl.multiple_of(owner * rows, rows), rows)
        return jnp.dot(spread[mine, :], prod[:, at], preferred_element_type=jnp.float32)

    def finish(strip, carry):
        at = pl.ds(pl.multiple_of(strip * 256, 256), 256)
        for dc in range(1, n_coarse):
            outgoing[dc - 1, strip] = contract(lax.rem(c + dc, n_coarse), at).astype(jnp.bfloat16)
            part_copy(dc, strip).start()
        return carry

    lax.fori_loop(0, strips, finish, 0)

    def own(strip, carry):
        at = pl.ds(pl.multiple_of(strip * 256, 256), 256)
        total[:, at] = contract(c, at)
        return carry

    lax.fori_loop(0, strips, own, 0)

    for strip in range(strips):
        for dc in range(1, n_coarse):
            part_copy(dc, strip).wait_recv()
        for half in range(2):
            j = strip * 2 + half
            value = total[:, j * 128:(j + 1) * 128]
            for dc in range(1, n_coarse):
                value = value + incoming[dc - 1, strip, :, half * 128:(half + 1) * 128].astype(jnp.float32)
            out_ref[pl.ds(j, rows, stride=columns // 128), :] = value

    for dc in range(1, n_coarse):
        for strip in range(strips):
            part_copy(dc, strip).wait_send()
    for df, dm in far:
        ghost_copy(lax.rem(f + df, n_fine), lax.rem(m + dm, n_comp), me).wait_send()


def on_device(shape, a_vals, a_cols, p_vals, p_cols, gp_cols, send_list):
    n_fine, n_coarse, n_comp, per_peer = shape
    block_rows, block, _ = a_vals.shape
    width = p_vals.shape[2]
    slots = gp_cols.shape[0]
    links = a_cols.shape[1]
    depth = block_rows * block
    columns = (NC + EXT) * block
    rows = NC * block // n_coarse
    strips = columns // 256
    peers = n_fine * n_comp
    vmem = pl.BlockSpec(memory_space=pltpu.VMEM)
    smem = pl.BlockSpec(memory_space=pltpu.SMEM)
    owned = pl.pallas_call(
        functools.partial(kernel, shape),
        out_shape=jax.ShapeDtypeStruct((rows * columns // 128, 128), jnp.float32),
        in_specs=[vmem, vmem, smem, smem, smem, smem],
        out_specs=vmem,
        scratch_shapes=[
            pltpu.VMEM((slots, block, width), jnp.bfloat16),
            pltpu.VMEM((block_rows + slots, block, width), jnp.bfloat16),
            pltpu.VMEM((2, width // 128, links * block, 128), jnp.float32),
            pltpu.VMEM((NC * block, depth), jnp.bfloat16),
            pltpu.VMEM((rows, columns), jnp.float32),
            pltpu.VMEM((depth, columns), jnp.bfloat16),
            pltpu.VMEM((n_coarse - 1, strips, rows, 256), jnp.bfloat16),
            pltpu.VMEM((n_coarse - 1, strips, rows, 256), jnp.bfloat16),
            pltpu.SemaphoreType.DMA((peers,)),
            pltpu.SemaphoreType.DMA((peers,)),
            pltpu.SemaphoreType.DMA((n_coarse - 1, strips)),
            pltpu.SemaphoreType.DMA((n_coarse - 1, strips)),
        ],
        compiler_params=pltpu.CompilerParams(
            collective_id=0, has_side_effects=True, vmem_limit_bytes=52 * 1024 * 1024
        ),
    )(a_vals, p_vals, a_cols, p_cols, gp_cols, send_list)
    return owned.reshape((1, rows, 1, columns))


def solution(mesh):
    n_fine, n_coarse, n_comp = (mesh.shape[axis] for axis in ("fine", "coarse", "comp"))

    def run(a_vals, a_cols, p_vals, p_cols, gp_cols, send_list):
        per_peer = gp_cols.shape[0] // (mesh.size * n_fine * n_comp)
        shape = (n_fine, n_coarse, n_comp, per_peer)
        split = ("fine", "coarse", "comp")
        return jax.shard_map(
            functools.partial(on_device, shape),
            mesh=mesh,
            in_specs=(
                P(split, None, None), P(split, None), P(split, None, None),
                P(split, None), P(split, None), P(split),
            ),
            out_specs=P("fine", "coarse", "comp", None),
            check_vma=False,
        )(a_vals, a_cols, p_vals, p_cols, gp_cols, send_list)

    return run
```
